32 devices in a mesh: section: 2 (over core), expert: 16 (over z, y, x).
Axes of the slice: x: 2, y: 2, z: 4, core: 2. Of those that a mesh axis runs over, the one named last changes fastest.
Arguments:
- hidden_in: bfloat16 [2, 2048, 2048], P('section', 'expert'), may hold values from -6 to 6
- target_rows: bfloat16 [2, 2048, 2048], P('section', 'expert'), may hold values from -6 to 6
- norm_gain: float32 [2048], replicated, may hold values from 0.25 to 1.75
- router_weight: bfloat16 [2048, 8], replicated, may hold values from -0.125 to 0.125
- w_up: bfloat16 [16, 2048, 2048], P('expert', None, 'section'), may hold values from -0.125 to 0.125
- w_down: bfloat16 [16, 2048, 2048], P('expert', 'section'), may hold values from -0.09375 to 0.09375
- routes: int32 [2, 2048, 2], P('section', 'expert'), may hold values from 0 to 7, all different within a row; in each aligned block of 128 rows (0 to 127, 128 to 255, ..., all dimensions but the last counted through in order) at most 48 rows name the same one
- pair_ids: int32 [2, 2048], P('section', 'expert'), may hold values from 0 to 63, never falling along the last dimension, each value on 1 to 96 neighbouring positions
Outputs:
- layer_out: bfloat16 [2, 2048, 2048], P('section', 'expert')
- dual_score: float32 [64], P(('section', 'expert'))
The draws below stay inside these ranges and needn't reach their ends.
Inputs may be any that keep to these rules, and one draw needn't show every extreme that they name: `routes`: within each aligned block of 128 rows of one direction no expert is named more than 48 times; the two experts of a row differ. `pair_ids`: never falling along each direction; every pair from 0 to 63 has 1 to 96 tokens in each direction.
All inputs are finite; a program needn't handle non-finite values.
Results may differ from the reference program's by a relative error of at most 0.014.
Values may be sent and summed in bfloat16 or wider, within the bound.
No kernel may reach another device: no remote copies, remote signals or barrier semaphores. Data moves between devices by JAX's collectives and lax.ppermute only.
A program may use at most 128 MiB of HBM per device.

```python
import math
import jax
import jax.numpy as jnp
import numpy as np
from jax import lax

D = 2048
FF = 4096
TOK_DEV = 128
MAX_LEN = 96
EXPERTS = 8
CAP = 48
TOKENS = 2048
PAIRS = 64
N_EXPERT = 16


def level_of(stream_key, extent, cuts, low, largest):
    loudness, own = 1.0, jax.random.fold_in(stream_key, 6)
    for dim, blocks in cuts:
        draws = jnp.exp(jax.random.uniform(jax.random.fold_in(own, dim), (blocks,), jnp.float32, low / len(cuts), largest / len(cuts)))
        loudness = loudness * jnp.repeat(draws, extent[dim] // blocks).reshape([-1 if axis == dim else 1 for axis in range(len(extent))])
    return loudness


def length_profile(number_of, total, limit, lean):
    loads = [(1 << 20) // math.isqrt(rank ** lean) + 1 for rank in range(2, number_of + 1)]
    spare, given = total - limit - (number_of - 1), [1] * (number_of - 1)
    while spare > 0:
        free = [i for i in range(number_of - 1) if given[i] < limit]
        mass, budget = sum([loads[i] for i in free]), spare
        for i in free:
            more = min(limit - given[i], max(1, budget * loads[i] // mass), spare)
            given[i] = given[i] + more
            spare = spare - more
    return np.array([limit] + given)


def uneven(stream_key, count, total, most, skew):
    if count == 2:
        one = jax.random.randint(stream_key, (), max(1, total - most), min(most, total - 1) + 1)
        return jnp.stack([one, total - one])
    lengths = jnp.asarray(length_profile(count, total, most, skew), jnp.int32)
    couples = (count - 1) // 2
    giver, sink = lengths[1:1 + 2 * couples:2], lengths[2:2 + 2 * couples:2]
    room = jnp.minimum(giver - 1, most - sink)
    moved = jax.random.randint(jax.random.fold_in(stream_key, 1), (couples,), 0, 1 << 20) % (room + 1)
    lengths = lengths.at[1:1 + 2 * couples:2].set(giver - moved).at[2:2 + 2 * couples:2].set(sink + moved)
    return lengths[jax.random.permutation(jax.random.fold_in(stream_key, 2), count)]


def shared_out(rng, own, number, rows, amount, top, limit, lean):
    ranking = jax.random.permutation(rng, amount)
    crowded, ordinary = load_shares(amount, rows * top, limit, lean, True), load_shares(amount, rows * top, limit, lean, False)
    places = jnp.arange(amount)

    def named(sizes, offset_by):
        used = int((sizes > 0).sum())
        fixed = max(1, used // 4)
        passed = fixed + (places - fixed + offset_by * (used - fixed)) % max(1, amount - fixed)
        return jnp.zeros((amount,), jnp.int32).at[ranking[jnp.where(places < fixed, places, passed)]].set(jnp.asarray(sizes, jnp.int32))

    sizes = jnp.where(number % 4 == 0, named(crowded, number // 4), named(ordinary, number - number // 4 - 1))
    mixed = jax.random.permutation(jax.random.fold_in(own, 3), amount)
    donor, receiver = mixed[0:amount // 2 * 2:2], mixed[1:amount // 2 * 2:2]
    slack = jnp.minimum(sizes[donor] - 1, limit - sizes[receiver]) // 2
    slack = jnp.where((donor == ranking[0]) | (receiver == ranking[0]) | (sizes[receiver] == 0), 0, jnp.maximum(slack, 0))
    passed = jax.random.randint(jax.random.fold_in(own, 4), (amount // 2,), 0, 1 << 20) % (slack + 1)
    sizes = sizes.at[donor].add(-passed).at[receiver].add(passed)
    labels = jnp.searchsorted(jnp.cumsum(sizes), jnp.arange(rows * top), side="right").astype(jnp.int32)
    grid = labels.reshape(top, rows).T
    grid = grid[jax.random.permutation(jax.random.fold_in(own, 1), rows)]
    offset_by = jax.random.randint(jax.random.fold_in(own, 2), (rows, 1), 0, top)
    return jnp.take_along_axis(grid, (jnp.arange(top)[None, :] + offset_by) % top, axis=1)


def load_shares(number_of, total, most, lean, full):
    portions = [(1 << 20) // math.isqrt(standing ** lean) + 1 for standing in range(1, number_of + 1)]
    largest = most if full else min(most, max(-(-total // number_of), total * portions[0] // sum(portions)))
    least = 1 if total - largest >= number_of - 1 else 0
    given, rest = [largest] + [least] * (number_of - 1), total - largest - least * (number_of - 1)
    while rest > 0:
        candidates = [i for i in range(1, number_of) if given[i] < largest] or [i for i in range(1, number_of) if given[i] < most]
        pool, left = sum([portions[i] for i in candidates]), rest
        for i in candidates:
            addition = min(most - given[i], max(1, left * portions[i] // pool), rest)
            given[i] = given[i] + addition
            rest = rest - addition
    return np.array(given)


def centred(rng, extent, scale, reach, pieces=(), kind=jnp.bfloat16):
    gain = level_of(rng, extent, pieces, -0.22, 0.18) if pieces else 1.0
    values = jax.random.normal(rng, extent, jnp.float32) * scale * gain
    return jnp.minimum(jnp.maximum(values, -reach), reach).astype(kind)


def setup_inputs(seed: int = 0) -> dict:
    splits = jax.random.split(jax.random.key(seed), 9)
    hidden_in = centred(splits[0], (2, TOKENS, D), 1.0, 6.0, ((0, 2), (1, 16)))
    target_rows = centred(splits[1], (2, TOKENS, D), 1.0, 6.0, ((0, 2), (1, 16)))
    norm_gain = jnp.clip(1.0 + 0.15 * jax.random.normal(splits[2], (D,), jnp.float32), 0.25, 1.75)
    router_weight = centred(splits[3], (D, EXPERTS), D ** -0.5, 0.125)
    w_up = centred(splits[4], (N_EXPERT, D, FF // 2), D ** -0.5, 0.125, ((0, 16), (2, 2)))
    w_down = centred(splits[5], (N_EXPERT, FF // 2, D), FF ** -0.5, 0.09375, ((0, 16), (1, 2)))
    routes_keys = jax.random.split(jax.random.fold_in(splits[6], 1), 2 * TOKENS // TOK_DEV)
    routes_turns = jax.random.permutation(jax.random.fold_in(splits[6], 3), 2 * TOKENS // TOK_DEV)
    routes = jax.vmap(lambda own, number: shared_out(jax.random.fold_in(splits[6], 2), own, number, TOK_DEV, EXPERTS, 2, CAP, 2))(routes_keys, routes_turns).reshape((2, TOKENS, 2))
    pair_ids = jax.vmap(lambda own: jnp.searchsorted(jnp.cumsum(uneven(own, PAIRS, TOKENS, MAX_LEN, 1)), jnp.arange(TOKENS), side="right"))(jax.random.split(splits[7], 2)).reshape((2, TOKENS)).astype(jnp.int32)
    return dict(hidden_in=hidden_in, target_rows=target_rows, norm_gain=norm_gain, router_weight=router_weight, w_up=w_up, w_down=w_down, routes=routes, pair_ids=pair_ids)


def normalize(values, norm_gain):
    center = lax.optimization_barrier(jnp.mean(values, axis=-1, keepdims=True))
    shifted = values - center
    spread = lax.optimization_barrier(jnp.mean(shifted * shifted, axis=-1, keepdims=True))
    return shifted * lax.rsqrt(spread + 1e-05) * norm_gain

def run_expert(operands):
    rows_in, up_pair, down_pair = operands
    result = jnp.zeros((rows_in.shape[0], down_pair.shape[-1]), jnp.float32)
    for half_index in range(2):
        hidden = jnp.maximum(jnp.dot(rows_in, up_pair[half_index], preferred_element_type=jnp.float32), 0.0).astype(jnp.bfloat16)
        result = result + jnp.dot(hidden, down_pair[half_index], preferred_element_type=jnp.float32)
    return result.astype(jnp.bfloat16)

def place_rows(source, targets):
    return jnp.zeros((EXPERTS * CAP, D), jnp.bfloat16).at[targets].set(source)

def take_rows(regrouped, targets):
    return regrouped[targets]

def reference(hidden_in, target_rows, norm_gain, router_weight, w_up, w_down, routes, pair_ids):
    rows_all = 2 * TOKENS
    blocks = rows_all // TOK_DEV
    flat_input = hidden_in.reshape(rows_all, D).astype(jnp.float32)
    normed = normalize(flat_input, norm_gain).astype(jnp.bfloat16)
    logits = jnp.dot(normed, router_weight, preferred_element_type=jnp.float32)
    chosen = routes.reshape(rows_all, 2)
    picked = jnp.take_along_axis(logits, chosen, axis=1)
    gate_one = 1.0 / (1.0 + jnp.exp(picked[:, 1] - picked[:, 0]))
    gate_two = 1.0 / (1.0 + jnp.exp(picked[:, 0] - picked[:, 1]))
    block_routes = chosen.reshape(blocks, 2 * TOK_DEV)
    onehot = (block_routes[:, :, None] == jnp.arange(EXPERTS, dtype=jnp.int32)[None, None, :]).astype(jnp.int32)
    before = jnp.cumsum(onehot, axis=1) - onehot
    slot_pos = lax.optimization_barrier(jnp.sum(before * onehot, axis=2))
    targets = (block_routes * CAP + slot_pos).astype(jnp.int32)
    source = jnp.repeat(normed.reshape(blocks, TOK_DEV, D), 2, axis=1)
    buffers = jax.vmap(place_rows)(source, targets)
    per_expert = buffers.reshape(blocks, EXPERTS, CAP, D).transpose(1, 0, 2, 3).reshape(EXPERTS, blocks * CAP, D)
    expert_out = lax.map(run_expert, (per_expert, w_up.reshape(EXPERTS, 2, D, FF // 2), w_down.reshape(EXPERTS, 2, FF // 2, D)))
    regrouped = expert_out.reshape(EXPERTS, blocks, CAP, D).transpose(1, 0, 2, 3).reshape(blocks, EXPERTS * CAP, D)
    gathered = jax.vmap(take_rows)(regrouped, targets).reshape(rows_all, 2, D).astype(jnp.float32)
    combined = flat_input + gate_one[:, None] * gathered[:, 0] + gate_two[:, None] * gathered[:, 1]
    layer_out = combined.astype(jnp.bfloat16)
    token_score = lax.optimization_barrier(jnp.sum(layer_out.astype(jnp.float32) * target_rows.reshape(rows_all, D).astype(jnp.float32), axis=1)) / math.sqrt(D)
    score_rows = token_score.reshape(2, TOKENS)
    totals = []
    counts = []
    for branch in range(2):
        totals.append(jax.ops.segment_sum(score_rows[branch], pair_ids[branch], num_segments=PAIRS))
        counts.append(jax.ops.segment_sum(jnp.ones((TOKENS,), jnp.float32), pair_ids[branch], num_segments=PAIRS))
    forward_entropy = -totals[0] / counts[0]
    backward_entropy = -totals[1] / counts[1]
    dual_score = jnp.abs(forward_entropy - backward_entropy) + 0.5 * (forward_entropy + backward_entropy)
    return (layer_out.reshape(2, TOKENS, D), dual_score)
```

```python
import math

import jax
import jax.numpy as jnp
from jax import lax
from jax.experimental import pallas as pl
from jax.experimental.pallas import tpu as pltpu
from jax.sharding import PartitionSpec as P

PAIR_DEV = 2
LANES = 128
MIB = 1 << 20
VMEM = pl.BlockSpec(memory_space=pltpu.VMEM)


def normalize(values, norm_gain):
    center = jnp.mean(values, axis=-1, keepdims=True)
    shifted = values - center
    spread = jnp.mean(shifted * shifted, axis=-1, keepdims=True)
    return shifted * lax.rsqrt(spread + 1e-05) * norm_gain


def row_sum(values):
    return jnp.sum(values, axis=1, keepdims=True)


def place_body(capacity, hidden, other, gain, router, routes, other_routes, *outs):
    sends, weights = outs[:-1], outs[-1]
    experts = router.shape[1]
    tok_rows = hidden.shape[0]
    couples = experts // 2
    slots = experts * capacity
    side = lax.axis_index("section")
    group = lax.axis_index("expert") // 2
    expert_ids = lax.broadcasted_iota(jnp.int32, (tok_rows, experts), 1)
    before = (
        lax.broadcasted_iota(jnp.int32, (tok_rows, tok_rows), 0)
        > lax.broadcasted_iota(jnp.int32, (tok_rows, tok_rows), 1)
    ).astype(jnp.bfloat16)
    columns = lax.broadcasted_iota(jnp.int32, (tok_rows, slots), 1)
    rows, placing = [], []
    for turn, (values, chosen) in enumerate(((hidden, routes), (other, other_routes))):
        normed = normalize(values[...].astype(jnp.float32), gain[...]).astype(jnp.bfloat16)
        chosen = chosen[...]
        named = [chosen[:, k : k + 1] == expert_ids for k in range(2)]
        member = jnp.where(named[0] | named[1], 1.0, 0.0).astype(jnp.bfloat16)
        earlier = jnp.dot(before, member, preferred_element_type=jnp.float32)
        place = [row_sum(jnp.where(n, earlier, 0.0)).astype(jnp.int32) for n in named]
        step = [chosen[:, k : k + 1] ^ group for k in range(2)]
        mine = [(k & 1) == side for k in step]
        full = [(k >> 1) * (2 * capacity) + p for k, p in zip(step, place)]
        target = [jnp.where(m, f + turn * capacity, -1) for m, f in zip(mine, full)]
        placing.append(
            jnp.where((columns == target[0]) | (columns == target[1]), 1.0, 0.0).astype(jnp.bfloat16)
        )
        rows.append(normed)
        if turn == 0:
            logits = jnp.dot(normed, router[...], preferred_element_type=jnp.float32)
            picked = [row_sum(jnp.where(n, logits, 0.0)) for n in named]
            gates = (
                1.0 / (1.0 + jnp.exp(picked[1] - picked[0])),
                1.0 / (1.0 + jnp.exp(picked[0] - picked[1])),
            )
            wide = lax.broadcasted_iota(jnp.int32, weights.shape, 1)
            back = [
                jnp.where(m, f, slots + (k >> 1) * capacity + p)
                for m, f, k, p in zip(mine, full, step, place)
            ]
            weights[...] = jnp.where(wide == back[0], gates[0], 0.0) + jnp.where(
                wide == back[1], gates[1], 0.0
            )
    sent = lax.dot_general(
        jnp.concatenate(placing, axis=0),
        jnp.concatenate(rows, axis=0),
        (((0,), (0,)), ((), ())),
        preferred_element_type=jnp.float32,
    ).astype(jnp.bfloat16)
    span = sends[0].shape[0]
    for k, ref in enumerate(sends):
        ref[...] = sent[k * span : (k + 1) * span]


def expert_body(own, across, up, down, up_other, down_other, kept, sent, rows, total):
    step = pl.program_id(0)
    span = own.shape[0]

    @pl.when(step == 0)
    def _():
        rows[:span] = own[...]
        rows[span:] = across[...]

    part = None
    for up_part, down_part in ((up, down), (up_other, down_other)):
        hidden = jnp.maximum(
            jnp.dot(rows[...], up_part[...], preferred_element_type=jnp.float32), 0.0
        ).astype(jnp.bfloat16)
        product = jnp.dot(hidden, down_part[...], preferred_element_type=jnp.float32)
        part = product if part is None else part + product

    @pl.when(step == 0)
    def _():
        total[...] = part

    @pl.when(step > 0)
    def _():
        total[...] += part

    @pl.when(step == pl.num_programs(0) - 1)
    def _():
        kept[...] = total[:span]
        sent[...] = total[span:].astype(jnp.bfloat16)


def expert_work(own, across, up, down, up_other, down_other):
    span, features = own.shape
    units = up.shape[1]
    block = min(256, units)
    rows_spec = pl.BlockSpec((span, features), lambda i: (0, 0))
    up_spec = pl.BlockSpec((features, block), lambda i: (0, i))
    down_spec = pl.BlockSpec((block, features), lambda i: (i, 0))
    return pl.pallas_call(
        expert_body,
        grid=(units // block,),
        in_specs=[rows_spec, rows_spec, up_spec, down_spec, up_spec, down_spec],
        out_specs=[rows_spec, rows_spec],
        out_shape=[
            jax.ShapeDtypeStruct((span, features), jnp.float32),
            jax.ShapeDtypeStruct((span, features), jnp.bfloat16),
        ],
        scratch_shapes=[
            pltpu.VMEM((2 * span, features), jnp.bfloat16),
            pltpu.VMEM((2 * span, features), jnp.float32),
        ],
        compiler_params=pltpu.CompilerParams(vmem_limit_bytes=32 * MIB),
        cost_estimate=pl.CostEstimate(
            flops=16 * span * features * units,
            bytes_accessed=8 * features * units,
            transcendentals=0,
        ),
    )(own, across, up, down, up_other, down_other)


def combine_body(rounds, pair_rows, *refs):
    returned, crossed = refs[:rounds], refs[rounds : 2 * rounds]
    weights, hidden, target, pairs, layer_out, sums = refs[2 * rounds :]
    features = hidden.shape[1]
    span, half = returned[0].shape[0], crossed[0].shape[0]
    gate = weights[...]
    high = gate.astype(jnp.bfloat16)
    low = (gate - high.astype(jnp.float32)).astype(jnp.bfloat16)
    total = hidden[...].astype(jnp.float32)
    rows = jnp.concatenate([r[...] for r in returned + crossed], axis=0)
    total = total + (
        jnp.dot(high, rows, preferred_element_type=jnp.float32)
        + jnp.dot(low, rows, preferred_element_type=jnp.float32)
    )
    result = total.astype(jnp.bfloat16)
    layer_out[...] = result
    score = row_sum(result.astype(jnp.float32) * target[...].astype(jnp.float32)) / math.sqrt(features)
    lane = lax.broadcasted_iota(jnp.int32, (score.shape[0], LANES), 1)
    owner = lax.broadcasted_iota(jnp.int32, (pair_rows, score.shape[0]), 0) * PAIR_DEV
    gathered = None
    for k in range(PAIR_DEV):
        belongs = jnp.where(pairs[...] == owner + k, 1.0, 0.0)
        column = jnp.where(lane == k, score, 0.0) + jnp.where(lane == PAIR_DEV + k, 1.0, 0.0)
        one = jnp.dot(
            belongs, column, preferred_element_type=jnp.float32, precision=lax.Precision.HIGHEST
        )
        gathered = one if gathered is None else gathered + one
    sums[...] = gathered


def local(hidden_in, target_rows, norm_gain, router_weight, w_up, w_down, routes, pair_ids):
    tok_rows = hidden_in.shape[1]
    features = hidden_in.shape[2]
    experts = router_weight.shape[1]
    capacity = 3 * tok_rows // experts
    sections, chips = lax.axis_size("section"), lax.axis_size("expert")
    couples = experts // 2
    rounds = min(4, couples)
    each = couples // rounds
    span = each * 2 * capacity
    both = ("section", "expert")

    def over_section(value):
        return lax.ppermute(value, "section", [(0, 1), (1, 0)])

    def over_x(value):
        return lax.ppermute(value, "expert", [(i, i ^ 1) for i in range(chips)])

    def over_groups(value, index):
        parts = []
        for k in range(each):
            couple = index * each + k
            pairs = [
                (side * chips + i, side * chips + (i ^ (2 * (2 * couple + side))))
                for side in range(sections)
                for i in range(chips)
            ]
            part = value[k * 2 * capacity : (k + 1) * 2 * capacity]
            parts.append(lax.ppermute(part, both, pairs))
        return parts[0] if each == 1 else jnp.concatenate(parts, axis=0)

    other_hidden = over_section(hidden_in[0])
    other_routes = over_section(routes[0])
    sends = pl.pallas_call(
        lambda *refs: place_body(capacity, *refs),
        in_specs=[VMEM] * 6,
        out_specs=[VMEM] * (rounds + 1),
        out_shape=[jax.ShapeDtypeStruct((span, features), jnp.bfloat16)] * rounds
        + [jax.ShapeDtypeStruct((tok_rows, experts * capacity * 3 // 2), jnp.float32)],
        compiler_params=pltpu.CompilerParams(vmem_limit_bytes=32 * MIB),
    )(hidden_in[0], other_hidden, norm_gain[None], router_weight, routes[0], other_routes)
    sends, weights = sends[:-1], sends[-1]
    up, down = w_up[0], w_down[0]
    up_other, down_other = over_section(up), over_section(down)

    order = list(range(rounds))
    order = [order[k] for k in (2, 3, 1, 0)] if rounds == 4 else order[::-1]
    arrived = {k: over_groups(sends[k], k) for k in order}
    returned, crossed = {}, {}
    for k in (0, 2, 1, 3) if rounds == 4 else order:
        across = over_x(arrived[k])
        kept, sent = expert_work(arrived[k], across, up, down, up_other, down_other)
        summed = (kept + over_x(sent).astype(jnp.float32)).astype(jnp.bfloat16)
        returned[k] = over_groups(summed, k)
        crossed[k] = over_section(
            returned[k].reshape(each, 2, capacity, features)[:, 1].reshape(each * capacity, features)
        )
    layer_out, sums = pl.pallas_call(
        lambda *refs: combine_body(rounds, sections * chips, *refs),
        in_specs=[VMEM] * (2 * rounds + 4),
        out_specs=[VMEM] * 2,
        out_shape=[
            jax.ShapeDtypeStruct((tok_rows, features), jnp.bfloat16),
            jax.ShapeDtypeStruct((sections * chips, LANES), jnp.float32),
        ],
        compiler_params=pltpu.CompilerParams(vmem_limit_bytes=32 * MIB),
    )(
        *[returned[k] for k in range(rounds)],
        *[crossed[k] for k in range(rounds)],
        weights,
        hidden_in[0],
        target_rows[0],
        pair_ids,
    )
    owned = lax.all_to_all(sums, both, split_axis=0, concat_axis=0, tiled=True)
    owned = jnp.sum(owned.reshape(sections, chips, LANES), axis=1)
    entropy = -owned[:, :PAIR_DEV] / owned[:, PAIR_DEV : 2 * PAIR_DEV]
    dual_score = jnp.abs(entropy[0] - entropy[1]) + 0.5 * (entropy[0] + entropy[1])
    return (layer_out[None], dual_score)


def solution(mesh):
    in_specs = (
        P("section", "expert", None),
        P("section", "expert", None),
        P(),
        P(),
        P("expert", None, "section"),
        P("expert", "section", None),
        P("section", "expert", None),
        P("section", "expert"),
    )
    out_specs = (P("section", "expert", None), P(("section", "expert")))
    return jax.shard_map(local, mesh=mesh, in_specs=in_specs, out_specs=out_specs, check_vma=False)
```

```python
import math

import jax
import jax.numpy as jnp
from jax import lax
from jax.experimental import pallas as pl
from jax.experimental.pallas import tpu as pltpu
from jax.sharding import PartitionSpec as P

PAIR_DEV = 2
LANES = 128
MIB = 1 << 20
VMEM = pl.BlockSpec(memory_space=pltpu.VMEM)


def normalize(values, norm_gain):
    center = jnp.mean(values, axis=-1, keepdims=True)
    shifted = values - center
    spread = jnp.mean(shifted * shifted, axis=-1, keepdims=True)
    return shifted * lax.rsqrt(spread + 1e-05) * norm_gain


def row_sum(values):
    return jnp.sum(values, axis=1, keepdims=True)


def column_sum(values):
    return jnp.sum(values, axis=0, keepdims=True)


def whole(shape):
    return pl.BlockSpec(shape, lambda i: (0, 0))


def after(value, *others):
    return lax.optimization_barrier((value, *others))[0] if others else value


def lay_out(capacity, turn, values, gain, routes):
    tok_rows = values.shape[0]
    experts = 3 * tok_rows // capacity
    side = lax.axis_index("section")
    group = lax.axis_index("expert") // 2
    normed = normalize(values[...].astype(jnp.float32), gain[...]).astype(jnp.bfloat16)
    expert_ids = lax.broadcasted_iota(jnp.int32, (experts, tok_rows), 0)
    before = jnp.where(
        lax.broadcasted_iota(jnp.int32, (tok_rows, tok_rows), 0)
        < lax.broadcasted_iota(jnp.int32, (tok_rows, tok_rows), 1),
        1.0,
        0.0,
    ).astype(jnp.bfloat16)
    chosen = [routes[k : k + 1, :] for k in range(2)]
    named = [c == expert_ids for c in chosen]
    member = jnp.where(named[0] | named[1], 1.0, 0.0).astype(jnp.bfloat16)
    earlier = jnp.dot(member, before, preferred_element_type=jnp.float32)
    place = [column_sum(jnp.where(n, earlier, 0.0)).astype(jnp.int32) for n in named]
    step = [c ^ group for c in chosen]
    mine = [(k & 1) == side for k in step]
    full = [(k >> 1) * (2 * capacity) + p for k, p in zip(step, place)]
    slots = lax.broadcasted_iota(jnp.int32, (experts * capacity, tok_rows), 0)
    target = [jnp.where(m, f + turn * capacity, -1) for m, f in zip(mine, full)]
    placing = jnp.where((slots == target[0]) | (slots == target[1]), 1.0, 0.0).astype(jnp.bfloat16)
    back = [
        jnp.where(m, f, experts * capacity + (k >> 1) * capacity + p)
        for m, f, k, p in zip(mine, full, step, place)
    ]
    return normed, placing, named, back


def own_body(capacity, hidden, gain, router, routes, rows, place, weights):
    normed, placing, named, back = lay_out(capacity, 0, hidden, gain, routes)
    rows[...] = normed
    place[...] = placing
    logits = lax.dot_general(
        router[...], normed, (((1,), (1,)), ((), ())), preferred_element_type=jnp.float32
    )
    picked = [column_sum(jnp.where(n, logits, 0.0)) for n in named]
    gates = (
        1.0 / (1.0 + jnp.exp(picked[1] - picked[0])),
        1.0 / (1.0 + jnp.exp(picked[0] - picked[1])),
    )
    wide = lax.broadcasted_iota(jnp.int32, weights.shape, 0)
    weights[...] = jnp.where(wide == back[0], gates[0], 0.0) + jnp.where(
        wide == back[1], gates[1], 0.0
    )


def place_body(capacity, rows, place, other, gain, routes, *sends):
    normed, placing, _, _ = lay_out(capacity, 1, other, gain, routes)
    sent = (
        jnp.dot(place[...], rows[...], preferred_element_type=jnp.float32)
        + jnp.dot(placing, normed, preferred_element_type=jnp.float32)
    ).astype(jnp.bfloat16)
    span = sends[0].shape[0]
    for k, ref in enumerate(sends):
        ref[...] = sent[k * span : (k + 1) * span]


def expert_body(own, across, up, down, up_other, down_other, kept, sent, rows, total):
    step = pl.program_id(0)
    span = own.shape[0]

    @pl.when(step == 0)
    def _():
        rows[:span] = own[...]
        rows[span:] = across[...]

    part = None
    for up_part, down_part in ((up, down), (up_other, down_other)):
        hidden = jnp.maximum(
            jnp.dot(rows[...], up_part[...], preferred_element_type=jnp.float32), 0.0
        ).astype(jnp.bfloat16)
        product = jnp.dot(hidden, down_part[...], preferred_element_type=jnp.float32)
        part = product if part is None else part + product

    @pl.when(step == 0)
    def _():
        total[...] = part

    @pl.when(step > 0)
    def _():
        total[...] += part

    @pl.when(step == pl.num_programs(0) - 1)
    def _():
        kept[...] = total[:span]
        sent[...] = total[span:].astype(jnp.bfloat16)


def expert_work(span, own, across, up, down, up_other, down_other):
    features = own[0].shape[1]
    units = up.shape[1]
    block = min(256, units)
    rows_spec = pl.BlockSpec((span, features), lambda i: (0, 0))
    up_spec = pl.BlockSpec((features, block), lambda i: (0, i))
    down_spec = pl.BlockSpec((block, features), lambda i: (i, 0))
    return pl.pallas_call(
        expert_body,
        grid=(units // block,),
        in_specs=[
            pl.BlockSpec((span, features), lambda i: (own[1], 0)),
            pl.BlockSpec((span, features), lambda i: (across[1], 0)),
            up_spec,
            down_spec,
            up_spec,
            down_spec,
        ],
        out_specs=[rows_spec, rows_spec],
        out_shape=[
            jax.ShapeDtypeStruct((span, features), jnp.float32),
            jax.ShapeDtypeStruct((span, features), jnp.bfloat16),
        ],
        scratch_shapes=[
            pltpu.VMEM((2 * span, features), jnp.bfloat16),
            pltpu.VMEM((2 * span, features), jnp.float32),
        ],
        compiler_params=pltpu.CompilerParams(vmem_limit_bytes=32 * MIB),
        cost_estimate=pl.CostEstimate(
            flops=16 * span * features * units,
            bytes_accessed=8 * features * units,
            transcendentals=0,
        ),
        name="expert",
    )(own[0], across[0], up, down, up_other, down_other)


def combine_body(rounds, pair_rows, *refs):
    returned, crossed = refs[:rounds], refs[rounds : 2 * rounds]
    weights, hidden, target, pairs, layer_out, sums = refs[2 * rounds :]
    features = hidden.shape[1]
    span, half = returned[0].shape[0], crossed[0].shape[0]
    gate = weights[...]
    high = gate.astype(jnp.bfloat16)
    low = (gate - high.astype(jnp.float32)).astype(jnp.bfloat16)
    total = hidden[...].astype(jnp.float32)
    rows = jnp.concatenate([r[...] for r in returned + crossed], axis=0)
    for part in (high, low):
        total = total + lax.dot_general(
            part, rows, (((0,), (0,)), ((), ())), preferred_element_type=jnp.float32
        )
    result = total.astype(jnp.bfloat16)
    layer_out[...] = result
    score = row_sum(result.astype(jnp.float32) * target[...].astype(jnp.float32)) / math.sqrt(features)
    lane = lax.broadcasted_iota(jnp.int32, (score.shape[0], LANES), 1)
    owner = lax.broadcasted_iota(jnp.int32, (pair_rows, score.shape[0]), 0) * PAIR_DEV
    gathered = None
    for k in range(PAIR_DEV):
        belongs = jnp.where(pairs[...] == owner + k, 1.0, 0.0)
        column = jnp.where(lane == k, score, 0.0) + jnp.where(lane == PAIR_DEV + k, 1.0, 0.0)
        one = jnp.dot(
            belongs, column, preferred_element_type=jnp.float32, precision=lax.Precision.HIGHEST
        )
        gathered = one if gathered is None else gathered + one
    sums[...] = gathered


def local(hidden_in, target_rows, norm_gain, router_weight, w_up, w_down, routes, pair_ids):
    tok_rows = hidden_in.shape[1]
    features = hidden_in.shape[2]
    experts = router_weight.shape[1]
    capacity = 3 * tok_rows // experts
    sections, chips = lax.axis_size("section"), lax.axis_size("expert")
    couples = experts // 2
    rounds = min(4, couples)
    each = couples // rounds
    span = each * 2 * capacity
    both = ("section", "expert")

    def over_section(value):
        return lax.ppermute(value, "section", [(0, 1), (1, 0)])

    def over_x(value):
        return lax.ppermute(value, "expert", [(i, i ^ 1) for i in range(chips)])

    def over_groups(value, index):
        parts = []
        for k in range(each):
            couple = index * each + k
            pairs = [
                (side * chips + i, side * chips + (i ^ (2 * (2 * couple + side))))
                for side in range(sections)
                for i in range(chips)
            ]
            part = value if each == 1 else value[k * 2 * capacity : (k + 1) * 2 * capacity]
            parts.append(lax.ppermute(part, both, pairs))
        return parts[0] if each == 1 else jnp.concatenate(parts, axis=0)

    rows_in, gain, router = hidden_in[0], norm_gain[None], router_weight.T
    chosen = routes[0].T
    other_rows = over_section(rows_in)
    other_routes = over_section(chosen)
    slots = experts * capacity
    normed, placing, weights = pl.pallas_call(
        lambda *refs: own_body(capacity, *refs),
        grid=(1,),
        in_specs=[whole(a.shape) for a in (rows_in, gain, router, chosen)],
        out_specs=[
            whole((tok_rows, features)),
            whole((slots, tok_rows)),
            whole((slots * 3 // 2, tok_rows)),
        ],
        out_shape=[
            jax.ShapeDtypeStruct((tok_rows, features), jnp.bfloat16),
            jax.ShapeDtypeStruct((slots, tok_rows), jnp.bfloat16),
            jax.ShapeDtypeStruct((slots * 3 // 2, tok_rows), jnp.float32),
        ],
        compiler_params=pltpu.CompilerParams(vmem_limit_bytes=16 * MIB),
        name="own_tokens",
    )(rows_in, gain, router, chosen)
    sends = pl.pallas_call(
        lambda *refs: place_body(capacity, *refs),
        in_specs=[VMEM] * 5,
        out_specs=[VMEM] * rounds,
        out_shape=[jax.ShapeDtypeStruct((span, features), jnp.bfloat16)] * rounds,
        compiler_params=pltpu.CompilerParams(vmem_limit_bytes=16 * MIB),
        cost_estimate=pl.CostEstimate(flops=6 * 10**9, bytes_accessed=10**6, transcendentals=0),
        name="place_rows",
    )(normed, placing, other_rows, gain, other_routes)
    up, down = w_up[0], w_down[0]
    up_other = over_section(after(up, other_rows, other_routes, normed))
    down_other = over_section(after(down, other_rows, other_routes, normed))

    last = rounds - 1
    arrived, across, kept, sent, halves, returned, crossed = {}, {}, {}, {}, {}, {}, {}

    def arrive(k, *others):
        arrived[k] = (over_groups(after(sends[k], *others), k), 0)

    def arrive_across_first(k):
        pair = jnp.concatenate([sends[k], over_x(sends[k])], axis=0)
        if each == 1:
            pair = over_groups(pair, k)
            arrived[k], across[k] = (pair, 0), (pair, 1)
        else:
            arrived[k] = (over_groups(pair[:span], k), 0)
            across[k] = (over_groups(pair[span:], k), 0)

    def exchange(k, *others):
        across[k] = (over_x(after(arrived[k][0], *others)), 0)

    def work(k, *others):
        own = (after(arrived[k][0], *others), arrived[k][1])
        kept[k], sent[k] = expert_work(span, own, across[k], up, down, up_other, down_other)

    def cross(k, *others):
        halves[k] = over_x(after(sent[k], *others))

    def give_back(k):
        summed = (kept[k] + halves[k].astype(jnp.float32)).astype(jnp.bfloat16)
        returned[k] = over_groups(summed, k)
        crossed[k] = over_section(
            returned[k].reshape(each, 2, capacity, features)[:, 1].reshape(each * capacity, features)
        )

    if rounds == 4:
        arrive(2)
        arrive(1)
        arrive(0)
        arrive(3)
        exchange(0)
        exchange(2)
        work(0)
        exchange(1, kept[0])
        cross(0)
        work(1, kept[0])
        exchange(3, kept[1])
        work(2, kept[1])
        cross(2)
        give_back(2)
        work(3, halves[2])
        cross(3)
        give_back(3)
        cross(1, halves[2])
        give_back(1)
        give_back(0)
    else:
        for k in range(rounds):
            arrive(k)
            exchange(k)
            work(k)
            cross(k)
            give_back(k)
    layer_out, sums = pl.pallas_call(
        lambda *refs: combine_body(rounds, sections * chips, *refs),
        in_specs=[VMEM] * (2 * rounds + 4),
        out_specs=[VMEM] * 2,
        out_shape=[
            jax.ShapeDtypeStruct((tok_rows, features), jnp.bfloat16),
            jax.ShapeDtypeStruct((sections * chips, LANES), jnp.float32),
        ],
        compiler_params=pltpu.CompilerParams(vmem_limit_bytes=32 * MIB),
    )(
        *[returned[k] for k in range(rounds)],
        *[crossed[k] for k in range(rounds)],
        weights,
        hidden_in[0],
        target_rows[0],
        pair_ids,
    )
    owned = lax.all_to_all(sums, both, split_axis=0, concat_axis=0, tiled=True)
    owned = jnp.sum(owned.reshape(sections, chips, LANES), axis=1)
    entropy = -owned[:, :PAIR_DEV] / owned[:, PAIR_DEV : 2 * PAIR_DEV]
    dual_score = jnp.abs(entropy[0] - entropy[1]) + 0.5 * (entropy[0] + entropy[1])
    return (layer_out[None], dual_score)


def solution(mesh):
    in_specs = (
        P("section", "expert", None),
        P("section", "expert", None),
        P(),
        P(),
        P("expert", None, "section"),
        P("expert", "section", None),
        P("section", "expert", None),
        P("section", "expert"),
    )
    out_specs = (P("section", "expert", None), P(("section", "expert")))
    return jax.shard_map(local, mesh=mesh, in_specs=in_specs, out_specs=out_specs, check_vma=False)
```

```python
import math

import jax
import jax.numpy as jnp
from jax import lax
from jax.experimental import pallas as pl
from jax.experimental.pallas import tpu as pltpu
from jax.sharding import PartitionSpec as P

PAIR_DEV = 2
LANES = 128
MIB = 1 << 20
VMEM = pl.BlockSpec(memory_space=pltpu.VMEM)


def normalize(values, norm_gain):
    center = jnp.mean(values, axis=-1, keepdims=True)
    shifted = values - center
    spread = jnp.mean(shifted * shifted, axis=-1, keepdims=True)
    return shifted * lax.rsqrt(spread + 1e-05) * norm_gain


def row_sum(values):
    return jnp.sum(values, axis=1, keepdims=True)


def column_sum(values):
    return jnp.sum(values, axis=0, keepdims=True)


def whole(shape):
    return pl.BlockSpec(shape, lambda i: (0, 0))


def after(value, *others):
    return lax.optimization_barrier((value, *others))[0] if others else value


def order_body(before):
    before[...] = jnp.where(
        lax.broadcasted_iota(jnp.int32, before.shape, 0)
        < lax.broadcasted_iota(jnp.int32, before.shape, 1),
        1.0,
        0.0,
    ).astype(jnp.bfloat16)


def lay_out(capacity, turn, values, gain, routes, before):
    tok_rows = values.shape[0]
    experts = 3 * tok_rows // capacity
    side = lax.axis_index("section")
    group = lax.axis_index("expert") // 2
    normed = normalize(values[...].astype(jnp.float32), gain[...]).astype(jnp.bfloat16)
    expert_ids = lax.broadcasted_iota(jnp.int32, (experts, tok_rows), 0)
    chosen = [routes[k : k + 1, :] for k in range(2)]
    named = [c == expert_ids for c in chosen]
    member = jnp.where(named[0] | named[1], 1.0, 0.0).astype(jnp.bfloat16)
    earlier = jnp.dot(member, before[...], preferred_element_type=jnp.float32)
    place = [column_sum(jnp.where(n, earlier, 0.0)).astype(jnp.int32) for n in named]
    step = [c ^ group for c in chosen]
    mine = [(k & 1) == side for k in step]
    full = [(k >> 1) * (2 * capacity) + p for k, p in zip(step, place)]
    slots = lax.broadcasted_iota(jnp.int32, (experts * capacity, tok_rows), 0)
    target = [jnp.where(m, f + turn * capacity, -1) for m, f in zip(mine, full)]
    placing = jnp.where((slots == target[0]) | (slots == target[1]), 1.0, 0.0).astype(jnp.bfloat16)
    back = [
        jnp.where(m, f, experts * capacity + (k >> 1) * capacity + p)
        for m, f, k, p in zip(mine, full, step, place)
    ]
    return normed, placing, named, back


def own_body(capacity, hidden, gain, router, routes, before, rows, place, weights, gain_out):
    gain_out[...] = gain[...]
    normed, placing, named, back = lay_out(capacity, 0, hidden, gain, routes, before)
    rows[...] = normed
    place[...] = placing
    logits = lax.dot_general(
        router[...], normed, (((1,), (1,)), ((), ())), preferred_element_type=jnp.float32
    )
    picked = [column_sum(jnp.where(n, logits, 0.0)) for n in named]
    gates = (
        1.0 / (1.0 + jnp.exp(picked[1] - picked[0])),
        1.0 / (1.0 + jnp.exp(picked[0] - picked[1])),
    )
    wide = lax.broadcasted_iota(jnp.int32, weights.shape, 0)
    weights[...] = jnp.where(wide == back[0], gates[0], 0.0) + jnp.where(
        wide == back[1], gates[1], 0.0
    )


def place_body(capacity, rows, place, other, gain, routes, before, *sends):
    normed, placing, _, _ = lay_out(capacity, 1, other, gain, routes, before)
    sent = (
        jnp.dot(place[...], rows[...], preferred_element_type=jnp.float32)
        + jnp.dot(placing, normed, preferred_element_type=jnp.float32)
    ).astype(jnp.bfloat16)
    span = sends[0].shape[0]
    for k, ref in enumerate(sends):
        ref[...] = sent[k * span : (k + 1) * span]


def expert_body(own, across, up, down, up_other, down_other, kept, sent, rows, total):
    step = pl.program_id(0)
    span = own.shape[0]

    @pl.when(step == 0)
    def _():
        rows[:span] = own[...]
        rows[span:] = across[...]

    part = None
    for up_part, down_part in ((up, down), (up_other, down_other)):
        hidden = jnp.maximum(
            jnp.dot(rows[...], up_part[...], preferred_element_type=jnp.float32), 0.0
        ).astype(jnp.bfloat16)
        product = jnp.dot(hidden, down_part[...], preferred_element_type=jnp.float32)
        part = product if part is None else part + product

    @pl.when(step == 0)
    def _():
        total[...] = part

    @pl.when(step > 0)
    def _():
        total[...] += part

    @pl.when(step == pl.num_programs(0) - 1)
    def _():
        kept[...] = total[:span]
        sent[...] = total[span:].astype(jnp.bfloat16)


def expert_work(span, own, across, up, down, up_other, down_other):
    features = own[0].shape[1]
    units = up.shape[1]
    block = min(512, units)
    rows_spec = pl.BlockSpec((span, features), lambda i: (0, 0))
    up_spec = pl.BlockSpec((features, block), lambda i: (0, i))
    down_spec = pl.BlockSpec((block, features), lambda i: (i, 0))
    return pl.pallas_call(
        expert_body,
        grid=(units // block,),
        in_specs=[
            pl.BlockSpec((span, features), lambda i: (own[1], 0)),
            pl.BlockSpec((span, features), lambda i: (across[1], 0)),
            up_spec,
            down_spec,
            up_spec,
            down_spec,
        ],
        out_specs=[rows_spec, rows_spec],
        out_shape=[
            jax.ShapeDtypeStruct((span, features), jnp.float32),
            jax.ShapeDtypeStruct((span, features), jnp.bfloat16),
        ],
        scratch_shapes=[
            pltpu.VMEM((2 * span, features), jnp.bfloat16),
            pltpu.VMEM((2 * span, features), jnp.float32),
        ],
        compiler_params=pltpu.CompilerParams(vmem_limit_bytes=32 * MIB),
        cost_estimate=pl.CostEstimate(
            flops=16 * span * features * units,
            bytes_accessed=8 * features * units,
            transcendentals=0,
        ),
        name="expert",
    )(own[0], across[0], up, down, up_other, down_other)


def combine_body(swapped, rounds, pair_rows, *refs):
    returned, crossed = refs[:rounds], refs[rounds:-6]
    weights, hidden, target, pairs, layer_out, sums = refs[-6:]
    features = hidden.shape[1]
    own = sum(r.shape[0] for r in returned)
    half = own // rounds // 2
    sources = [weights[:own]] + [weights[own + k * half : own + (k + 1) * half] for k in swapped]
    gate = jnp.concatenate(sources, axis=0)
    high = gate.astype(jnp.bfloat16)
    low = (gate - high.astype(jnp.float32)).astype(jnp.bfloat16)
    total = hidden[...].astype(jnp.float32)
    rows = jnp.concatenate([r[...] for r in returned + crossed], axis=0)
    for part in (high, low):
        total = total + lax.dot_general(
            part, rows, (((0,), (0,)), ((), ())), preferred_element_type=jnp.float32
        )
    result = total.astype(jnp.bfloat16)
    layer_out[...] = result
    score = row_sum(result.astype(jnp.float32) * target[...].astype(jnp.float32)) / math.sqrt(features)
    lane = lax.broadcasted_iota(jnp.int32, (score.shape[0], LANES), 1)
    owner = lax.broadcasted_iota(jnp.int32, (pair_rows, score.shape[0]), 0) * PAIR_DEV
    gathered = None
    for k in range(PAIR_DEV):
        belongs = jnp.where(pairs[...] == owner + k, 1.0, 0.0)
        column = jnp.where(lane == k, score, 0.0) + jnp.where(lane == PAIR_DEV + k, 1.0, 0.0)
        one = jnp.dot(
            belongs, column, preferred_element_type=jnp.float32, precision=lax.Precision.HIGHEST
        )
        gathered = one if gathered is None else gathered + one
    sums[...] = gathered


def local(hidden_in, target_rows, norm_gain, router_weight, w_up, w_down, routes, pair_ids):
    tok_rows = hidden_in.shape[1]
    features = hidden_in.shape[2]
    experts = router_weight.shape[1]
    capacity = 3 * tok_rows // experts
    sections, chips = lax.axis_size("section"), lax.axis_size("expert")
    couples = experts // 2
    rounds = min(4, couples)
    each = couples // rounds
    span = each * 2 * capacity
    both = ("section", "expert")

    def over_section(value):
        return lax.ppermute(value, "section", [(0, 1), (1, 0)])

    def over_x(value):
        return lax.ppermute(value, "expert", [(i, i ^ 1) for i in range(chips)])

    def over_groups(value, index):
        parts = []
        for k in range(each):
            couple = index * each + k
            pairs = [
                (side * chips + i, side * chips + (i ^ (2 * (2 * couple + side))))
                for side in range(sections)
                for i in range(chips)
            ]
            part = value if each == 1 else value[k * 2 * capacity : (k + 1) * 2 * capacity]
            parts.append(lax.ppermute(part, both, pairs))
        return parts[0] if each == 1 else jnp.concatenate(parts, axis=0)

    rows_in, gain, router = hidden_in[0], norm_gain[None], router_weight.T
    chosen = routes[0].T
    other_rows = over_section(rows_in)
    other_routes = over_section(chosen)
    slots = experts * capacity
    before = pl.pallas_call(
        order_body,
        out_specs=VMEM,
        out_shape=jax.ShapeDtypeStruct((tok_rows, tok_rows), jnp.bfloat16),
        compiler_params=pltpu.CompilerParams(vmem_limit_bytes=16 * MIB),
        cost_estimate=pl.CostEstimate(flops=2 * 10**9, bytes_accessed=10**6, transcendentals=0),
        name="token_order",
    )()
    normed, placing, weights, gain = pl.pallas_call(
        lambda *refs: own_body(capacity, *refs),
        in_specs=[VMEM] * 5,
        out_specs=[VMEM] * 4,
        out_shape=[
            jax.ShapeDtypeStruct((tok_rows, features), jnp.bfloat16),
            jax.ShapeDtypeStruct((slots, tok_rows), jnp.bfloat16),
            jax.ShapeDtypeStruct((slots * 3 // 2, tok_rows), jnp.float32),
            jax.ShapeDtypeStruct(gain.shape, jnp.float32),
        ],
        compiler_params=pltpu.CompilerParams(vmem_limit_bytes=16 * MIB),
        name="own_tokens",
    )(rows_in, gain, router, chosen, before)
    sends = pl.pallas_call(
        lambda *refs: place_body(capacity, *refs),
        in_specs=[VMEM] * 6,
        out_specs=[VMEM] * rounds,
        out_shape=[jax.ShapeDtypeStruct((span, features), jnp.bfloat16)] * rounds,
        compiler_params=pltpu.CompilerParams(vmem_limit_bytes=16 * MIB),
        cost_estimate=pl.CostEstimate(flops=6 * 10**9, bytes_accessed=10**6, transcendentals=0),
        name="place_rows",
    )(normed, placing, other_rows, gain, other_routes, before)
    up, down = w_up[0], w_down[0]
    up_other = over_section(after(up, other_rows, other_routes, normed))

    last = rounds - 1
    down_other = over_section(after(down, other_rows, other_routes, normed))

    arrived, across, kept, sent, halves, returned = {}, {}, {}, {}, {}, {}
    crossed, swapped = [], []

    def arrive(k, *others):
        arrived[k] = (over_groups(after(sends[k], *others), k), 0)

    def arrive_across_first(k):
        pair = jnp.concatenate([sends[k], over_x(sends[k])], axis=0)
        if each == 1:
            pair = over_groups(pair, k)
            arrived[k], across[k] = (pair, 0), (pair, 1)
        else:
            arrived[k] = (over_groups(pair[:span], k), 0)
            across[k] = (over_groups(pair[span:], k), 0)

    def exchange(k, *others):
        across[k] = (over_x(after(arrived[k][0], *others)), 0)

    def work(k, *others):
        own = (after(arrived[k][0], *others), arrived[k][1])
        kept[k], sent[k] = expert_work(span, own, across[k], up, down, up_other, down_other)

    def cross(k, *others):
        halves[k] = over_x(after(sent[k], *others))

    def give_back(k):
        summed = (kept[k] + halves[k].astype(jnp.float32)).astype(jnp.bfloat16)
        returned[k] = over_groups(summed, k)

    def swap(ks, *others):
        halves_out = [
            returned[k].reshape(each, 2, capacity, features)[:, 1].reshape(each * capacity, features)
            for k in ks
        ]
        value = halves_out[0] if len(ks) == 1 else jnp.concatenate(halves_out, axis=0)
        crossed.append(over_section(after(value, *others)))
        swapped.extend(ks)

    if rounds == 4:
        arrive(2)
        arrive(1)
        arrive(0)
        arrive(3)
        exchange(0)
        exchange(2)
        work(0)
        exchange(1, kept[0])
        cross(0)
        work(1, kept[0])
        exchange(3, kept[1])
        work(2, kept[1])
        cross(2)
        give_back(2)
        work(3, halves[2])
        cross(3)
        give_back(3)
        cross(1, halves[2])
        give_back(1)
        give_back(0)
        swap((0,), halves[1], halves[3])
        swap((2,), halves[1], halves[3])
        swap((3,))
        swap((1,))
    else:
        for k in range(rounds):
            arrive(k)
            exchange(k)
            work(k)
            cross(k)
            give_back(k)
            swap((k,))
    layer_out, sums = pl.pallas_call(
        lambda *refs: combine_body(swapped, rounds, sections * chips, *refs),
        in_specs=[VMEM] * (rounds + len(crossed) + 4),
        out_specs=[VMEM] * 2,
        out_shape=[
            jax.ShapeDtypeStruct((tok_rows, features), jnp.bfloat16),
            jax.ShapeDtypeStruct((sections * chips, LANES), jnp.float32),
        ],
        compiler_params=pltpu.CompilerParams(vmem_limit_bytes=32 * MIB),
    )(
        *[returned[k] for k in range(rounds)],
        *crossed,
        weights,
        hidden_in[0],
        target_rows[0],
        pair_ids,
    )
    owned = lax.all_to_all(sums, both, split_axis=0, concat_axis=0, tiled=True)
    owned = jnp.sum(owned.reshape(sections, chips, LANES), axis=1)
    entropy = -owned[:, :PAIR_DEV] / owned[:, PAIR_DEV : 2 * PAIR_DEV]
    dual_score = jnp.abs(entropy[0] - entropy[1]) + 0.5 * (entropy[0] + entropy[1])
    return (layer_out[None], dual_score)


def solution(mesh):
    in_specs = (
        P("section", "expert", None),
        P("section", "expert", None),
        P(),
        P(),
        P("expert", None, "section"),
        P("expert", "section", None),
        P("section", "expert", None),
        P("section", "expert"),
    )
    out_specs = (P("section", "expert", None), P(("section", "expert")))
    return jax.shard_map(local, mesh=mesh, in_specs=in_specs, out_specs=out_specs, check_vma=False)
```

```python
import math

import jax
import jax.numpy as jnp
from jax import lax
from jax.experimental import pallas as pl
from jax.experimental.pallas import tpu as pltpu
from jax.sharding import PartitionSpec as P

PAIR_DEV = 2
LANES = 128
MIB = 1 << 20
VMEM = pl.BlockSpec(memory_space=pltpu.VMEM)


def normalize(values, norm_gain):
    center = jnp.mean(values, axis=-1, keepdims=True)
    shifted = values - center
    spread = jnp.mean(shifted * shifted, axis=-1, keepdims=True)
    return shifted * lax.rsqrt(spread + 1e-05) * norm_gain


def row_sum(values):
    return jnp.sum(values, axis=1, keepdims=True)


def column_sum(values):
    return jnp.sum(values, axis=0, keepdims=True)


def whole(shape):
    return pl.BlockSpec(shape, lambda i: (0, 0))


def after(value, *others):
    return lax.optimization_barrier((value, *others))[0] if others else value


def order_body(before):
    before[...] = jnp.where(
        lax.broadcasted_iota(jnp.int32, before.shape, 0)
        < lax.broadcasted_iota(jnp.int32, before.shape, 1),
        1.0,
        0.0,
    ).astype(jnp.bfloat16)


def lay_out(capacity, turn, values, gain, routes, before):
    tok_rows = values.shape[0]
    experts = 3 * tok_rows // capacity
    side = lax.axis_index("section")
    group = lax.axis_index("expert") // 2
    normed = normalize(values[...].astype(jnp.float32), gain[...]).astype(jnp.bfloat16)
    expert_ids = lax.broadcasted_iota(jnp.int32, (experts, tok_rows), 0)
    chosen = [routes[k : k + 1, :] for k in range(2)]
    named = [c == expert_ids for c in chosen]
    member = jnp.where(named[0] | named[1], 1.0, 0.0).astype(jnp.bfloat16)
    earlier = jnp.dot(member, before[...], preferred_element_type=jnp.float32)
    place = [column_sum(jnp.where(n, earlier, 0.0)).astype(jnp.int32) for n in named]
    step = [c ^ group for c in chosen]
    mine = [(k & 1) == side for k in step]
    full = [(k >> 1) * (2 * capacity) + p for k, p in zip(step, place)]
    slots = lax.broadcasted_iota(jnp.int32, (experts * capacity, tok_rows), 0)
    target = [jnp.where(m, f + turn * capacity, -1) for m, f in zip(mine, full)]
    placing = jnp.where((slots == target[0]) | (slots == target[1]), 1.0, 0.0).astype(jnp.bfloat16)
    back = [
        jnp.where(m, f, experts * capacity + (k >> 1) * capacity + p)
        for m, f, k, p in zip(mine, full, step, place)
    ]
    return normed, placing, named, back


def own_body(capacity, hidden, gain, router, routes, before, rows, place, weights, gain_out):
    gain_out[...] = gain[...]
    normed, placing, named, back = lay_out(capacity, 0, hidden, gain, routes, before)
    rows[...] = normed
    place[...] = placing
    logits = lax.dot_general(
        router[...], normed, (((1,), (1,)), ((), ())), preferred_element_type=jnp.float32
    )
    picked = [column_sum(jnp.where(n, logits, 0.0)) for n in named]
    gates = (
        1.0 / (1.0 + jnp.exp(picked[1] - picked[0])),
        1.0 / (1.0 + jnp.exp(picked[0] - picked[1])),
    )
    wide = lax.broadcasted_iota(jnp.int32, weights.shape, 0)
    weights[...] = jnp.where(wide == back[0], gates[0], 0.0) + jnp.where(
        wide == back[1], gates[1], 0.0
    )


def place_body(capacity, rows, place, other, gain, routes, before, *sends):
    normed, placing, _, _ = lay_out(capacity, 1, other, gain, routes, before)
    sent = (
        jnp.dot(place[...], rows[...], preferred_element_type=jnp.float32)
        + jnp.dot(placing, normed, preferred_element_type=jnp.float32)
    ).astype(jnp.bfloat16)
    span = sends[0].shape[0]
    for k, ref in enumerate(sends):
        ref[...] = sent[k * span : (k + 1) * span]


def expert_body(own, across, up, down, up_other, down_other, kept, sent, rows, total):
    step = pl.program_id(0)
    span = own.shape[0]

    @pl.when(step == 0)
    def _():
        rows[:span] = own[...]
        rows[span:] = across[...]

    part = None
    for up_part, down_part in ((up, down), (up_other, down_other)):
        hidden = jnp.maximum(
            jnp.dot(rows[...], up_part[...], preferred_element_type=jnp.float32), 0.0
        ).astype(jnp.bfloat16)
        product = jnp.dot(hidden, down_part[...], preferred_element_type=jnp.float32)
        part = product if part is None else part + product

    @pl.when(step == 0)
    def _():
        total[...] = part

    @pl.when(step > 0)
    def _():
        total[...] += part

    @pl.when(step == pl.num_programs(0) - 1)
    def _():
        kept[...] = total[:span]
        sent[...] = total[span:].astype(jnp.bfloat16)


def expert_work(span, own, across, up, down, up_other, down_other):
    features = own[0].shape[1]
    units = up.shape[1]
    block = min(512, units)
    rows_spec = pl.BlockSpec((span, features), lambda i: (0, 0))
    up_spec = pl.BlockSpec((features, block), lambda i: (0, i))
    down_spec = pl.BlockSpec((block, features), lambda i: (i, 0))
    return pl.pallas_call(
        expert_body,
        grid=(units // block,),
        in_specs=[
            pl.BlockSpec((span, features), lambda i: (own[1], 0)),
            pl.BlockSpec((span, features), lambda i: (across[1], 0)),
            up_spec,
            down_spec,
            up_spec,
            down_spec,
        ],
        out_specs=[rows_spec, rows_spec],
        out_shape=[
            jax.ShapeDtypeStruct((span, features), jnp.float32),
            jax.ShapeDtypeStruct((span, features), jnp.bfloat16),
        ],
        scratch_shapes=[
            pltpu.VMEM((2 * span, features), jnp.bfloat16),
            pltpu.VMEM((2 * span, features), jnp.float32),
        ],
        compiler_params=pltpu.CompilerParams(vmem_limit_bytes=32 * MIB),
        cost_estimate=pl.CostEstimate(
            flops=16 * span * features * units,
            bytes_accessed=8 * features * units,
            transcendentals=0,
        ),
        name="expert",
    )(own[0], across[0], up, down, up_other, down_other)


def combine_body(swapped, rounds, pair_rows, *refs):
    returned, crossed = refs[:rounds], refs[rounds:-6]
    weights, hidden, target, pairs, layer_out, sums = refs[-6:]
    features = hidden.shape[1]
    own = sum(r.shape[0] for r in returned)
    half = own // rounds // 2
    sources = [weights[:own]] + [weights[own + k * half : own + (k + 1) * half] for k in swapped]
    gate = jnp.concatenate(sources, axis=0)
    high = gate.astype(jnp.bfloat16)
    low = (gate - high.astype(jnp.float32)).astype(jnp.bfloat16)
    total = hidden[...].astype(jnp.float32)
    rows = jnp.concatenate([r[...] for r in returned + crossed], axis=0)
    for part in (high, low):
        total = total + lax.dot_general(
            part, rows, (((0,), (0,)), ((), ())), preferred_element_type=jnp.float32
        )
    result = total.astype(jnp.bfloat16)
    layer_out[...] = result
    score = row_sum(result.astype(jnp.float32) * target[...].astype(jnp.float32)) / math.sqrt(features)
    lane = lax.broadcasted_iota(jnp.int32, (score.shape[0], LANES), 1)
    owner = lax.broadcasted_iota(jnp.int32, (pair_rows, score.shape[0]), 0) * PAIR_DEV
    gathered = None
    for k in range(PAIR_DEV):
        belongs = jnp.where(pairs[...] == owner + k, 1.0, 0.0)
        column = jnp.where(lane == k, score, 0.0) + jnp.where(lane == PAIR_DEV + k, 1.0, 0.0)
        one = jnp.dot(
            belongs, column, preferred_element_type=jnp.float32, precision=lax.Precision.HIGHEST
        )
        gathered = one if gathered is None else gathered + one
    sums[...] = gathered


def local(hidden_in, target_rows, norm_gain, router_weight, w_up, w_down, routes, pair_ids):
    tok_rows = hidden_in.shape[1]
    features = hidden_in.shape[2]
    experts = router_weight.shape[1]
    capacity = 3 * tok_rows // experts
    sections, chips = lax.axis_size("section"), lax.axis_size("expert")
    couples = experts // 2
    rounds = min(4, couples)
    each = couples // rounds
    span = each * 2 * capacity
    both = ("section", "expert")

    def over_section(value):
        return lax.ppermute(value, "section", [(0, 1), (1, 0)])

    def over_x(value):
        return lax.ppermute(value, "expert", [(i, i ^ 1) for i in range(chips)])

    def over_groups(value, index, flip=0):
        parts = []
        for k in range(each):
            couple = index * each + k
            pairs = [
                (side * chips + i, side * chips + (i ^ (2 * (2 * couple + side)) ^ flip))
                for side in range(sections)
                for i in range(chips)
            ]
            part = value if each == 1 else value[k * 2 * capacity : (k + 1) * 2 * capacity]
            parts.append(lax.ppermute(part, both, pairs))
        return parts[0] if each == 1 else jnp.concatenate(parts, axis=0)

    rows_in, gain, router = hidden_in[0], norm_gain[None], router_weight.T
    chosen = routes[0].T
    other_rows = over_section(rows_in)
    other_routes = over_section(chosen)
    slots = experts * capacity
    before = pl.pallas_call(
        order_body,
        out_specs=VMEM,
        out_shape=jax.ShapeDtypeStruct((tok_rows, tok_rows), jnp.bfloat16),
        compiler_params=pltpu.CompilerParams(vmem_limit_bytes=16 * MIB),
        cost_estimate=pl.CostEstimate(flops=2 * 10**9, bytes_accessed=10**6, transcendentals=0),
        name="token_order",
    )()
    normed, placing, weights, gain = pl.pallas_call(
        lambda *refs: own_body(capacity, *refs),
        in_specs=[VMEM] * 5,
        out_specs=[VMEM] * 4,
        out_shape=[
            jax.ShapeDtypeStruct((tok_rows, features), jnp.bfloat16),
            jax.ShapeDtypeStruct((slots, tok_rows), jnp.bfloat16),
            jax.ShapeDtypeStruct((slots * 3 // 2, tok_rows), jnp.float32),
            jax.ShapeDtypeStruct(gain.shape, jnp.float32),
        ],
        compiler_params=pltpu.CompilerParams(vmem_limit_bytes=16 * MIB),
        name="own_tokens",
    )(rows_in, gain, router, chosen, before)
    sends = pl.pallas_call(
        lambda *refs: place_body(capacity, *refs),
        in_specs=[VMEM] * 6,
        out_specs=[VMEM] * rounds,
        out_shape=[jax.ShapeDtypeStruct((span, features), jnp.bfloat16)] * rounds,
        compiler_params=pltpu.CompilerParams(vmem_limit_bytes=16 * MIB),
        cost_estimate=pl.CostEstimate(flops=6 * 10**9, bytes_accessed=10**6, transcendentals=0),
        name="place_rows",
    )(normed, placing, other_rows, gain, other_routes, before)
    up, down = w_up[0], w_down[0]
    up_other = over_section(after(up, other_rows, other_routes, normed))

    last = rounds - 1
    down_other = over_section(after(down, other_rows, other_routes, normed))

    arrived, across, kept, sent, halves, returned = {}, {}, {}, {}, {}, {}
    crossed, swapped = [], []

    def arrive(k, *others):
        arrived[k] = (over_groups(after(sends[k], *others), k), 0)

    def arrive_across(k, *others):
        across[k] = (over_groups(after(sends[k], *others), k, flip=1), 0)

    def exchange(k, *others):
        across[k] = (over_x(after(arrived[k][0], *others)), 0)

    def work(k, *others):
        own = (after(arrived[k][0], *others), arrived[k][1])
        kept[k], sent[k] = expert_work(span, own, across[k], up, down, up_other, down_other)

    def cross(k, *others):
        halves[k] = over_x(after(sent[k], *others))

    def give_back_straight(k, *others):
        near = over_groups(after(kept[k].astype(jnp.bfloat16), *others), k)
        far = over_groups(after(sent[k], *others), k, flip=1)
        returned[k] = (near.astype(jnp.float32) + far.astype(jnp.float32)).astype(jnp.bfloat16)

    def give_back(k):
        summed = (kept[k] + halves[k].astype(jnp.float32)).astype(jnp.bfloat16)
        returned[k] = over_groups(summed, k)

    def swap(ks, *others):
        halves_out = [
            returned[k].reshape(each, 2, capacity, features)[:, 1].reshape(each * capacity, features)
            for k in ks
        ]
        value = halves_out[0] if len(ks) == 1 else jnp.concatenate(halves_out, axis=0)
        crossed.append(over_section(after(value, *others)))
        swapped.extend(ks)

    if rounds == 4:
        arrive(2)
        arrive(1)
        arrive(0)
        arrive_across(0)
        arrive(3)
        exchange(2)
        work(0)
        exchange(1, kept[0])
        give_back_straight(0)
        work(1, kept[0])
        exchange(3, kept[1])
        work(2, kept[1])
        cross(2)
        give_back(2)
        work(3, halves[2])
        cross(3)
        give_back(3)
        cross(1, halves[2])
        give_back(1)
        swap((0,), halves[3])
        swap((2,), halves[3])
        swap((1,), halves[3])
        swap((3,))
    else:
        for k in range(rounds):
            arrive(k)
            exchange(k)
            work(k)
            cross(k)
            give_back(k)
            swap((k,))
    layer_out, sums = pl.pallas_call(
        lambda *refs: combine_body(swapped, rounds, sections * chips, *refs),
        in_specs=[VMEM] * (rounds + len(crossed) + 4),
        out_specs=[VMEM] * 2,
        out_shape=[
            jax.ShapeDtypeStruct((tok_rows, features), jnp.bfloat16),
            jax.ShapeDtypeStruct((sections * chips, LANES), jnp.float32),
        ],
        compiler_params=pltpu.CompilerParams(vmem_limit_bytes=32 * MIB),
    )(
        *[returned[k] for k in range(rounds)],
        *crossed,
        weights,
        hidden_in[0],
        target_rows[0],
        pair_ids,
    )
    owned = lax.all_to_all(sums, both, split_axis=0, concat_axis=0, tiled=True)
    owned = jnp.sum(owned.reshape(sections, chips, LANES), axis=1)
    entropy = -owned[:, :PAIR_DEV] / owned[:, PAIR_DEV : 2 * PAIR_DEV]
    dual_score = jnp.abs(entropy[0] - entropy[1]) + 0.5 * (entropy[0] + entropy[1])
    return (layer_out[None], dual_score)


def solution(mesh):
    in_specs = (
        P("section", "expert", None),
        P("section", "expert", None),
        P(),
        P(),
        P("expert", None, "section"),
        P("expert", "section", None),
        P("section", "expert", None),
        P("section", "expert"),
    )
    out_specs = (P("section", "expert", None), P(("section", "expert")))
    return jax.shard_map(local, mesh=mesh, in_specs=in_specs, out_specs=out_specs, check_vma=False)
```
